32 devices in a mesh: groups: 2 (over x), replica: 16 (over z, y, core).
Axes of the slice: x: 2, y: 2, z: 4, core: 2. Of those that a mesh axis runs over, the one named last changes fastest.
Arguments:
- hidden: bfloat16 [64, 28672], P('groups', 'replica'), parts along dimension 0, may hold values from -6 to 6
- down_matrix: bfloat16 [28672, 8192], P('replica'), may hold values from -0.03125 to 0.03125
- adapter_shrink: bfloat16 [32, 16, 28672], P('replica'), may hold values from -0.03125 to 0.03125
- adapter_expand: bfloat16 [32, 16, 8192], P('replica'), may hold values from -1.5 to 1.5
- row_adapter_index: int32 [64], P('groups'), parts along dimension 0, may hold values from 0 to 31
- slot_adapter_index: int32 [32], replicated, may hold values from 0 to 31, each once
Outputs:
- projected: bfloat16 [64, 8192], P(('groups', 'replica')), parts along dimension 0
The draws below stay inside these ranges and needn't reach their ends.
There are 2 independent parts, one for each index of `groups`. The reference program is written for one: setup_inputs(seed, part) draws one part's arguments, and reference() takes and returns one part's arrays. A program takes and returns all parts, laid end to end along the dimension named above; an argument that names none is the same for every part. Nothing has to cross between parts.
Inputs may be any that keep to these rules, and one draw needn't show every extreme that they name: `slot_adapter_index`: each adapter id stands in exactly one bank slot. `row_adapter_index`: every id names an adapter of the bank.
All inputs are finite; a program needn't handle non-finite values.
Results may differ from the reference program's by a relative error of at most 0.0044.
Values may be sent and summed in bfloat16 or wider, within the bound.
A program may use at most 128 MiB of HBM per device.

```python
import math
import jax
import jax.numpy as jnp
import numpy as np

MODEL_WIDTH = 8192
FEEDFORWARD_UNITS = 28672
ADAPTER_RANK = 16
ADAPTER_COUNT = 32
TOKENS = 32


def with_ends(drawn, stream_key, low, top_value):
    longest = drawn.shape.index(max(drawn.shape))
    spots = []
    for shift in (0, 1):
        where = [jax.random.randint(jax.random.fold_in(stream_key, axis), (), 0, length) for axis, length in enumerate(drawn.shape)]
        where[longest] = (where[longest] + shift) % drawn.shape[longest]
        spots.append(tuple(where))
    return drawn.at[spots[0]].set(low).at[spots[1]].set(top_value)


def raised(drawn, stream_key, source, target, parts, factor):
    def block_of(dim):
        return (jnp.arange(drawn.shape[dim]) // (drawn.shape[dim] // parts)).reshape((-1,) + (1,) * (drawn.ndim - 1 - dim))

    one_side = jax.random.permutation(stream_key, parts)[block_of(target)]
    far = (block_of(target) + parts // 2) % parts
    return jnp.where((block_of(source) == one_side) | (block_of(source) == far), factor * drawn, drawn)


def level_of(key, shape, pieces, low, high):
    level, own = 1.0, jax.random.fold_in(key, 6)
    for dim, shards_of in pieces:
        heights = jnp.exp(jax.random.uniform(jax.random.fold_in(own, dim), (shards_of,), jnp.float32, low / len(pieces), high / len(pieces)))
        level = level * jnp.repeat(heights, shape[dim] // shards_of).reshape([-1 if axis == dim else 1 for axis in range(len(shape))])
    return level


def rank_bounds(amount, slope):
    portions = [(1 << 20) // math.isqrt(grade ** slope) + 1 for grade in range(1, amount + 1)]
    scale = 1 + sum(portions) // (1 << 30)
    return np.cumsum(np.array([max(1, weight // scale) for weight in portions]))


def ranked(key, shape, number_of, slope):
    table = rank_bounds(number_of, slope)
    ticket = jax.random.randint(jax.random.fold_in(key, 1), shape, 0, int(table[number_of - 1]))
    standing = jnp.searchsorted(jnp.asarray(table, jnp.int32), ticket, side="right")
    return jax.random.permutation(jax.random.fold_in(key, 2), number_of)[standing].astype(jnp.int32)


def scatter_about(key, extent, spread, most, pieces=(), held_as=jnp.bfloat16):
    values = spread * jax.random.normal(key, extent, jnp.float32)
    if pieces:
        values = values * level_of(key, extent, pieces, -0.22, 0.18)
    return jnp.clip(values, -most, most).astype(held_as)


def bell_draw_with(stream_key, shape, scale, limit, split, heavy, held_as=jnp.bfloat16):
    drawn = scale * jax.random.normal(stream_key, shape, jnp.float32)
    if split:
        drawn = drawn * level_of(stream_key, shape, split, -0.22, 0.18)
    return jnp.clip(raised(drawn, jax.random.fold_in(stream_key, 3), *heavy), -limit, limit).astype(held_as)


def setup_inputs(seed: int = 0, part: int = 0) -> dict:
    streams_of = jax.random.split(jax.random.key(seed), 7)
    part_splits = jax.random.split(jax.random.fold_in(streams_of[6], part), 7)
    return {
        "hidden": bell_draw_with(part_splits[0], (TOKENS, FEEDFORWARD_UNITS), 1.0, 6.0, ((1, 16),), (1, 0, 16, 2.0)),
        "down_matrix": scatter_about(streams_of[1], (FEEDFORWARD_UNITS, MODEL_WIDTH), FEEDFORWARD_UNITS ** -0.5, 0.03125, ((0, 16),)),
        "adapter_shrink": scatter_about(streams_of[2], (ADAPTER_COUNT, ADAPTER_RANK, FEEDFORWARD_UNITS), FEEDFORWARD_UNITS ** -0.5, 0.03125, ((0, 16),)),
        "adapter_expand": scatter_about(streams_of[3], (ADAPTER_COUNT, ADAPTER_RANK, MODEL_WIDTH), ADAPTER_RANK ** -0.5, 1.5, ((0, 16),)),
        "row_adapter_index": with_ends(ranked(part_splits[4], (TOKENS,), ADAPTER_COUNT, 2), jax.random.fold_in(part_splits[4], 3), 0, ADAPTER_COUNT - 1).astype(jnp.int32),
        "slot_adapter_index": jax.random.permutation(streams_of[5], ADAPTER_COUNT).astype(jnp.int32),
    }


def reference(hidden, down_matrix, adapter_shrink, adapter_expand, row_adapter_index, slot_adapter_index):
    match = (row_adapter_index[:, None] == slot_adapter_index[None, :]).astype(jnp.float32)
    flattened_shrink = adapter_shrink.reshape(ADAPTER_COUNT * ADAPTER_RANK, FEEDFORWARD_UNITS)
    every_slot = jnp.dot(hidden, flattened_shrink.T, preferred_element_type=jnp.float32).reshape(TOKENS, ADAPTER_COUNT, ADAPTER_RANK)
    shrunk = jnp.sum(match[:, :, None] * every_slot, axis=1)
    scattered_rows = (match[:, :, None] * shrunk[:, None, :]).astype(jnp.bfloat16).reshape(TOKENS, ADAPTER_COUNT * ADAPTER_RANK)
    adapter_delta = jnp.dot(scattered_rows, adapter_expand.reshape(ADAPTER_COUNT * ADAPTER_RANK, MODEL_WIDTH), preferred_element_type=jnp.float32)
    base = jnp.dot(hidden, down_matrix, preferred_element_type=jnp.float32)
    return (base + adapter_delta).astype(jnp.bfloat16)
```

```python
import jax
import jax.numpy as jnp
from jax import lax
from jax.sharding import PartitionSpec as P


def on_device(
    hidden, down_matrix, adapter_shrink, adapter_expand, row_adapter_index, slot_adapter_index
):
    slots, rank, units = adapter_shrink.shape
    rows = hidden.shape[0]
    own_lanes = slots * rank
    gathered = lax.all_gather(hidden, "replica", axis=1, tiled=True)
    base = jnp.dot(hidden, down_matrix, preferred_element_type=jnp.float32)
    shrunk = lax.dot_general(
        gathered,
        adapter_shrink.reshape(own_lanes, units),
        (((1,), (1,)), ((), ())),
        preferred_element_type=jnp.float32,
    )
    first_slot = lax.axis_index("replica") * slots
    own_slots = lax.dynamic_slice_in_dim(slot_adapter_index, first_slot, slots, 0)
    match = row_adapter_index[:, None] == jnp.repeat(own_slots, rank)[None, :]
    spread = jnp.where(match, shrunk, 0.0).astype(jnp.bfloat16)
    delta = jnp.dot(
        spread,
        adapter_expand.reshape(own_lanes, adapter_expand.shape[2]),
        preferred_element_type=jnp.float32,
    )
    result = lax.psum_scatter(base + delta, "replica", scatter_dimension=0, tiled=True)
    return result.astype(jnp.bfloat16)


def solution(mesh):
    in_specs = (
        P("groups", "replica"),
        P("replica", None),
        P("replica", None, None),
        P("replica", None, None),
        P("groups"),
        P(),
    )
    out_specs = P(("groups", "replica"), None)
    return jax.shard_map(
        on_device, mesh=mesh, in_specs=in_specs, out_specs=out_specs, check_vma=False
    )
```

```python
import functools

import jax
import jax.numpy as jnp
from jax import lax
from jax.experimental import pallas as pl
from jax.experimental.pallas import tpu as pltpu
from jax.sharding import PartitionSpec as P

MESH = pl.DeviceIdType.MESH
F32 = jnp.float32
BF16 = jnp.bfloat16
NT = (((1,), (1,)), ((), ()))


def plain_on_device(
    hidden, down_matrix, adapter_shrink, adapter_expand, row_adapter_index, slot_adapter_index
):
    slots, rank, units = adapter_shrink.shape
    own_lanes = slots * rank
    gathered = lax.all_gather(hidden, "replica", axis=1, tiled=True)
    base = jnp.dot(hidden, down_matrix, preferred_element_type=F32)
    shrunk = lax.dot_general(
        gathered, adapter_shrink.reshape(own_lanes, units), NT, preferred_element_type=F32
    )
    first_slot = lax.axis_index("replica") * slots
    own_slots = lax.dynamic_slice_in_dim(slot_adapter_index, first_slot, slots, 0)
    match = row_adapter_index[:, None] == jnp.repeat(own_slots, rank)[None, :]
    spread = jnp.where(match, shrunk, 0.0).astype(BF16)
    delta = jnp.dot(
        spread,
        adapter_expand.reshape(own_lanes, adapter_expand.shape[2]),
        preferred_element_type=F32,
    )
    result = lax.psum_scatter(base + delta, "replica", scatter_dimension=0, tiled=True)
    return result.astype(BF16)


def kernel(
    nz, rank, slots,
    row_ref, slot_ref, hidden_ref, down_ref, shrink_ref, expand_ref, out_ref,
    dbuf, gath, shr, exp, own_acc, base_send, base_recv, s_acc, s_send, s_recv,
    vbuf, rs_send, rs_recv,
    d_sem, shl_sem, shs_sem, shr_sem, ex_sem, g_send, g_recv, b_send, b_recv, s_sem,
    r_send, r_recv,
):
    rows, width = hidden_ref.shape
    chips = 2 * nz
    nc, _, cw = dbuf.shape
    lanes = slots * rank
    half = rows // 2
    rep = lax.axis_index("replica")
    z = rep // 4
    y = (rep // 2) % 2
    core = rep % 2
    chip = rep // 2
    sibling = rep + 1 - 2 * core

    def to(device, src, dst, send, recv):
        return pltpu.make_async_remote_copy(
            src_ref=src, dst_ref=dst, send_sem=send, recv_sem=recv,
            device_id={"replica": device}, device_id_type=MESH,
        )

    def down_copy(n):
        start = n * cw if isinstance(n, int) else pl.multiple_of(n * cw, cw)
        return pltpu.make_async_copy(down_ref.at[:, pl.ds(start, cw)], dbuf.at[n], d_sem.at[n])

    def units_of(m, c):
        return pl.ds(pl.multiple_of((2 * m + c) * width, 128), width)

    def shrink_local(m):
        return pltpu.make_async_copy(
            shrink_ref.at[:, units_of(m, core)], shr.at[m, pl.ds(0, lanes)], shl_sem.at[m]
        )

    def shrink_remote(m):
        return to(
            sibling, shrink_ref.at[:, units_of(m, 1 - core)],
            shr.at[m, pl.ds(lanes, lanes)], shs_sem.at[m], shr_sem.at[m],
        )

    expand_local = pltpu.make_async_copy(expand_ref, exp.at[pl.ds(0, lanes)], ex_sem.at[0])
    expand_remote = to(sibling, expand_ref, exp.at[pl.ds(lanes, lanes)], ex_sem.at[1], ex_sem.at[2])

    for n in range(nc):
        down_copy(n).start()
    gath[chip] = hidden_ref[...]

    barrier = pltpu.get_barrier_semaphore()
    pl.semaphore_signal(barrier, inc=1, device_id={"replica": sibling}, device_id_type=MESH)
    for k in range(1, chips):
        other = lax.rem(chip + k, chips) * 2 + core
        pl.semaphore_signal(barrier, inc=1, device_id={"replica": other}, device_id_type=MESH)
    pl.semaphore_wait(barrier, chips)

    def g_copy(which, z0, yy):
        block = z0 * 2 + yy
        device = rep + 4 if which == 0 else rep - 4 if which == 1 else rep + 2 - 4 * y
        return to(
            device, gath.at[block], gath.at[block], g_send.at[which, z0], g_recv.at[block]
        )

    def when(condition, what):
        @pl.when(condition)
        def _():
            what()

    when(z < nz - 1, lambda: g_copy(0, z, y).start())
    when(z > 0, lambda: g_copy(1, z, y).start())
    g_copy(2, z, y).start()

    for m in range(chips):
        shrink_remote(m).start()
        shrink_local(m).start()
    expand_remote.start()
    expand_local.start()

    at = lax.broadcasted_iota(jnp.int32, (rows, rows), 0)
    token = lax.broadcasted_iota(jnp.int32, (rows, rows), 1)
    of_core = jnp.where(at < half, core, 1 - core)
    pair = jnp.where(at < half, at, at - half)
    order = (token == 4 * (pair >> 1) + 2 * of_core + (pair & 1)).astype(F32).astype(BF16)
    ordered = jnp.dot(order, hidden_ref[...], preferred_element_type=F32).astype(BF16)

    def base_copy(n):
        return to(sibling, base_send.at[n], base_recv.at[n], b_send.at[n], b_recv.at[n])

    def base_chunk(n):
        down_copy(n).wait()
        product = jnp.dot(ordered, dbuf[n], preferred_element_type=F32)
        own_acc[n] = product[:half]
        base_send[n] = product[half:]
        base_copy(n).start()

    def forward(distance):
        def from_below():
            z0 = z - distance
            g_copy(0, z0, y).wait_recv()
            when(z < nz - 1, lambda: g_copy(0, z0, y).start())
            g_copy(2, z0, y).start()

        def from_above():
            z0 = z + distance
            g_copy(1, z0, y).wait_recv()
            when(z > 0, lambda: g_copy(1, z0, y).start())
            g_copy(2, z0, y).start()

        when(z >= distance, from_below)
        when(z + distance < nz, from_above)

    def shrunk_block(m):
        shrink_local(m).wait()
        shrink_remote(m).wait_recv()
        s_acc[...] += lax.dot_general(shr[m], gath[m], NT, preferred_element_type=F32)

    s_acc[...] = jnp.zeros_like(s_acc)
    per = nc // nz
    for step in range(nz):
        lax.fori_loop(step * per, (step + 1) * per, lambda n, c: (base_chunk(n), c)[1], 0)
        if step < nz - 1:
            forward(step + 1)

    for z0 in range(nz):
        shrunk_block(z0 * 2 + y)
    across = [z, z + 1 - 2 * (z % 2), (z + 2) % 4, 3 - z]
    for z0 in across:
        g_copy(2, z0, 1 - y).wait_recv()
        shrunk_block(z0 * 2 + 1 - y)

    s_send[...] = jnp.zeros_like(s_send)
    s_send[:, :rows] = s_acc[...]
    s_copy = to(sibling, s_send, s_recv, s_sem.at[0], s_sem.at[1])
    s_copy.start()
    for n in range(nc):
        base_copy(n).wait_recv()
        own_acc[n] = own_acc[n] + base_recv[n]
    expand_local.wait()
    expand_remote.wait_recv()
    s_copy.wait_recv()
    own_sum = s_acc[:lanes] + s_recv[lanes:, :rows]
    sib_sum = s_acc[lanes:] + s_recv[:lanes, :rows]
    shrunk = jnp.concatenate([own_sum, sib_sum], axis=0)
    lane = lax.broadcasted_iota(jnp.int32, (2 * lanes, rows), 0)
    slot = jnp.zeros((2 * lanes, rows), jnp.int32)
    for k in range(slots):
        slot = jnp.where((lane >= k * rank) & (lane < (k + 1) * rank), slot_ref[rep * slots + k], slot)
        slot = jnp.where(
            (lane >= lanes + k * rank) & (lane < lanes + (k + 1) * rank),
            slot_ref[sibling * slots + k], slot,
        )
    spread = jnp.where(slot == row_ref[...], shrunk, 0.0).astype(BF16)
    own_spread = lax.dot_general(
        order[:half], spread, NT, preferred_element_type=F32
    ).astype(BF16)

    def finish(n, c):
        columns = pl.ds(pl.multiple_of(n * cw, cw), cw)
        delta = jnp.dot(own_spread, exp[:, columns], preferred_element_type=F32)
        vbuf[n] = (own_acc[n] + delta).astype(BF16)
        return c

    lax.fori_loop(0, nc, finish, 0)

    size = nc * half
    to_row = lax.broadcasted_iota(jnp.int32, (size, size), 0)
    from_row = lax.broadcasted_iota(jnp.int32, (size, size), 1)
    wanted = ((to_row >> 1) & 7) * 16 + (to_row >> 4) * 2 + (to_row & 1)
    shuffle = (from_row == wanted).astype(F32).astype(BF16)
    moved = jnp.dot(shuffle, vbuf[...].reshape(size, cw), preferred_element_type=F32)
    rs_send[...] = moved.astype(BF16).reshape(chips, half, cw)

    def rs_copy(k):
        other = lax.rem(chip + k, chips)
        return to(
            other * 2 + core, rs_send.at[other], rs_recv.at[chip], r_send.at[k], r_recv.at[chip]
        )

    for k in range(1, chips):
        rs_copy(k).start()
    total = rs_send[chip].astype(F32)
    for k in range(1, chips):
        source = lax.rem(chip + k, chips)
        to(sibling, rs_send.at[source], rs_recv.at[source], r_send.at[k], r_recv.at[source]).wait_recv()
        total = total + rs_recv[source].astype(F32)
    for q in range(nc):
        out_ref[:, q * cw:(q + 1) * cw] = total[2 * q:2 * q + 2].astype(BF16)

    for k in range(1, chips):
        rs_copy(k).wait_send()
    s_copy.wait_send()
    expand_remote.wait_send()
    for m in range(chips):
        shrink_remote(m).wait_send()
    for n in range(nc):
        base_copy(n).wait_send()
    for z0 in range(nz):
        when((z0 <= z) & (z < nz - 1), lambda: g_copy(0, z0, y).wait_send())
        when((z0 >= z) & (z > 0), lambda: g_copy(1, z0, y).wait_send())
        g_copy(2, z0, y).wait_send()


def fused_on_device(
    nz, hidden, down_matrix, adapter_shrink, adapter_expand, row_adapter_index, slot_adapter_index
):
    slots, rank, units = adapter_shrink.shape
    rows, width = hidden.shape
    model = down_matrix.shape[1]
    chips = 2 * nz
    lanes = slots * rank
    nc = chips
    cw = model // nc
    half = rows // 2
    vmem = pl.BlockSpec(memory_space=pltpu.VMEM)
    anywhere = pl.BlockSpec(memory_space=pl.ANY)
    dma = pltpu.SemaphoreType.DMA
    return pl.pallas_call(
        functools.partial(kernel, nz, rank, slots),
        out_shape=jax.ShapeDtypeStruct((rows // (2 * chips), model), BF16),
        in_specs=[
            vmem, pl.BlockSpec(memory_space=pltpu.SMEM), vmem, anywhere, anywhere, anywhere,
        ],
        out_specs=vmem,
        scratch_shapes=[
            pltpu.VMEM((nc, width, cw), BF16),
            pltpu.VMEM((chips, rows, width), BF16),
            pltpu.VMEM((chips, 2 * lanes, width), BF16),
            pltpu.VMEM((2 * lanes, model), BF16),
            pltpu.VMEM((nc, half, cw), F32),
            pltpu.VMEM((nc, half, cw), F32),
            pltpu.VMEM((nc, half, cw), F32),
            pltpu.VMEM((2 * lanes, rows), F32),
            pltpu.VMEM((2 * lanes, 128), F32),
            pltpu.VMEM((2 * lanes, 128), F32),
            pltpu.VMEM((nc, half, cw), BF16),
            pltpu.VMEM((chips, half, cw), BF16),
            pltpu.VMEM((chips, half, cw), BF16),
            dma((nc,)), dma((chips,)), dma((chips,)), dma((chips,)), dma((3,)),
            dma((3, nz)), dma((chips,)), dma((nc,)), dma((nc,)), dma((2,)),
            dma((chips,)), dma((chips,)),
        ],
        compiler_params=pltpu.CompilerParams(
            collective_id=0, has_side_effects=True, vmem_limit_bytes=56 * 1024 * 1024
        ),
    )(
        row_adapter_index.reshape(1, rows),
        slot_adapter_index,
        hidden,
        down_matrix,
        adapter_shrink.reshape(lanes, units),
        adapter_expand.reshape(lanes, model),
    )


def solution(mesh):
    replicas = mesh.shape["replica"]
    in_specs = (
        P("groups", "replica"),
        P("replica", None),
        P("replica", None, None),
        P("replica", None, None),
        P("groups"),
        P(),
    )
    out_specs = P(("groups", "replica"), None)
    body = functools.partial(fused_on_device, 4) if replicas == 16 else plain_on_device
    return jax.shard_map(
        body, mesh=mesh, in_specs=in_specs, out_specs=out_specs, check_vma=False
    )
```

```python
import functools

import jax
import jax.numpy as jnp
from jax import lax
from jax.experimental import pallas as pl
from jax.experimental.pallas import tpu as pltpu
from jax.sharding import PartitionSpec as P

MESH = pl.DeviceIdType.MESH
F32 = jnp.float32
BF16 = jnp.bfloat16
NT = (((1,), (1,)), ((), ()))


def plain_on_device(
    hidden, down_matrix, adapter_shrink, adapter_expand, row_adapter_index, slot_adapter_index
):
    slots, rank, units = adapter_shrink.shape
    own_lanes = slots * rank
    gathered = lax.all_gather(hidden, "replica", axis=1, tiled=True)
    base = jnp.dot(hidden, down_matrix, preferred_element_type=F32)
    shrunk = lax.dot_general(
        gathered, adapter_shrink.reshape(own_lanes, units), NT, preferred_element_type=F32
    )
    first_slot = lax.axis_index("replica") * slots
    own_slots = lax.dynamic_slice_in_dim(slot_adapter_index, first_slot, slots, 0)
    match = row_adapter_index[:, None] == jnp.repeat(own_slots, rank)[None, :]
    spread = jnp.where(match, shrunk, 0.0).astype(BF16)
    delta = jnp.dot(
        spread,
        adapter_expand.reshape(own_lanes, adapter_expand.shape[2]),
        preferred_element_type=F32,
    )
    result = lax.psum_scatter(base + delta, "replica", scatter_dimension=0, tiled=True)
    return result.astype(BF16)


def kernel(
    nz, rank, slots,
    row_ref, slot_ref, hidden_hbm, down_ref, shrink_ref, expand_ref, out_ref,
    dbuf, gath, shr, exp, own_acc, base_send, base_recv, s_acc, s_send, s_recv,
    vbuf, rs_send, rs_recv,
    in_sem, d_sem, shl_sem, shs_sem, shr_sem, ex_sem, g_send, g_recv, b_send, b_recv, s_sem,
    r_send, r_recv,
):
    rows, width = hidden_hbm.shape
    chips = 2 * nz
    nc, _, cw = dbuf.shape
    lanes = slots * rank
    half = rows // 2
    rep = lax.axis_index("replica")
    z = rep // 4
    y = (rep // 2) % 2
    core = rep % 2
    chip = rep // 2
    sibling = rep + 1 - 2 * core

    def to(device, src, dst, send, recv):
        return pltpu.make_async_remote_copy(
            src_ref=src, dst_ref=dst, send_sem=send, recv_sem=recv,
            device_id={"replica": device}, device_id_type=MESH,
        )

    def down_copy(n):
        start = n * cw if isinstance(n, int) else pl.multiple_of(n * cw, cw)
        return pltpu.make_async_copy(down_ref.at[:, pl.ds(start, cw)], dbuf.at[n], d_sem.at[n])

    def units_of(m, c):
        return pl.ds(pl.multiple_of((2 * m + c) * width, 128), width)

    def shrink_local(m):
        return pltpu.make_async_copy(
            shrink_ref.at[:, units_of(m, core)], shr.at[m, pl.ds(0, lanes)], shl_sem.at[m]
        )

    def shrink_remote(m):
        return to(
            sibling, shrink_ref.at[:, units_of(m, 1 - core)],
            shr.at[m, pl.ds(lanes, lanes)], shs_sem.at[m], shr_sem.at[m],
        )

    expand_local = pltpu.make_async_copy(expand_ref, exp.at[pl.ds(0, lanes)], ex_sem.at[0])
    expand_remote = to(sibling, expand_ref, exp.at[pl.ds(lanes, lanes)], ex_sem.at[1], ex_sem.at[2])

    barrier = pltpu.get_barrier_semaphore()
    pl.semaphore_signal(barrier, inc=1, device_id={"replica": sibling}, device_id_type=MESH)
    across_y = rep + 2 - 4 * y
    pl.semaphore_signal(barrier, inc=1, device_id={"replica": across_y}, device_id_type=MESH)

    @pl.when(z > 0)
    def _():
        pl.semaphore_signal(barrier, inc=1, device_id={"replica": rep - 4}, device_id_type=MESH)

    @pl.when(z < nz - 1)
    def _():
        pl.semaphore_signal(barrier, inc=1, device_id={"replica": rep + 4}, device_id_type=MESH)

    hidden_copy = pltpu.make_async_copy(hidden_hbm, gath.at[chip], in_sem.at[0])
    hidden_copy.start()
    for n in range(nc):
        down_copy(n).start()
    hidden_copy.wait()
    inner = (z > 0) & (z < nz - 1)

    @pl.when(inner)
    def _():
        pl.semaphore_wait(barrier, 4)

    @pl.when(jnp.logical_not(inner))
    def _():
        pl.semaphore_wait(barrier, 3)


    def g_copy(which, z0, yy):
        block = z0 * 2 + yy
        device = rep + 4 if which == 0 else rep - 4 if which == 1 else rep + 2 - 4 * y
        return to(
            device, gath.at[block], gath.at[block], g_send.at[which, z0], g_recv.at[block]
        )

    def when(condition, what):
        @pl.when(condition)
        def _():
            what()

    when(z < nz - 1, lambda: g_copy(0, z, y).start())
    when(z > 0, lambda: g_copy(1, z, y).start())
    g_copy(2, z, y).start()

    for m in range(chips):
        shrink_remote(m).start()
        shrink_local(m).start()
    expand_remote.start()
    expand_local.start()

    at = lax.broadcasted_iota(jnp.int32, (rows, rows), 0)
    token = lax.broadcasted_iota(jnp.int32, (rows, rows), 1)
    of_core = jnp.where(at < half, core, 1 - core)
    pair = jnp.where(at < half, at, at - half)
    order = (token == 4 * (pair >> 1) + 2 * of_core + (pair & 1)).astype(F32).astype(BF16)
    ordered = jnp.dot(order, gath[chip], preferred_element_type=F32).astype(BF16)

    def base_copy(n):
        return to(sibling, base_send.at[n], base_recv.at[n], b_send.at[n], b_recv.at[n])

    def base_chunk(n):
        down_copy(n).wait()
        product = jnp.dot(ordered, dbuf[n], preferred_element_type=F32)
        own_acc[n] = product[:half]
        base_send[n] = product[half:]
        base_copy(n).start()

    def forward(distance):
        def from_below():
            z0 = z - distance
            g_copy(0, z0, y).wait_recv()
            when(z < nz - 1, lambda: g_copy(0, z0, y).start())
            g_copy(2, z0, y).start()
            shrunk_block(z0 * 2 + y)

        def from_above():
            z0 = z + distance
            g_copy(1, z0, y).wait_recv()
            when(z > 0, lambda: g_copy(1, z0, y).start())
            g_copy(2, z0, y).start()
            shrunk_block(z0 * 2 + y)

        when(z >= distance, from_below)
        when(z + distance < nz, from_above)

    def shrunk_block(m):
        shrink_local(m).wait()
        shrink_remote(m).wait_recv()
        s_acc[...] += lax.dot_general(shr[m], gath[m], NT, preferred_element_type=F32)

    def shrunk_across(k):
        z0 = (z, z + 1 - 2 * (z % 2), (z + 2) % 4, 3 - z)[k]
        g_copy(2, z0, 1 - y).wait_recv()
        shrunk_block(z0 * 2 + 1 - y)

    s_acc[...] = jnp.zeros_like(s_acc)
    per = nc // nz
    for step in range(nz):
        lax.fori_loop(step * per, (step + 1) * per, lambda n, c: (base_chunk(n), c)[1], 0)
        if step < nz - 1:
            forward(step + 1)
        if step == 0:
            shrunk_block(chip)
        else:
            shrunk_across(step - 1)
    shrunk_across(nz - 1)

    s_send[...] = jnp.zeros_like(s_send)
    s_send[:, :rows] = s_acc[...]
    s_copy = to(sibling, s_send, s_recv, s_sem.at[0], s_sem.at[1])
    s_copy.start()
    lane = lax.broadcasted_iota(jnp.int32, (2 * lanes, rows), 0)
    slot = jnp.zeros((2 * lanes, rows), jnp.int32)
    for k in range(slots):
        slot = jnp.where((lane >= k * rank) & (lane < (k + 1) * rank), slot_ref[rep * slots + k], slot)
        slot = jnp.where(
            (lane >= lanes + k * rank) & (lane < lanes + (k + 1) * rank),
            slot_ref[sibling * slots + k], slot,
        )
    size = nc * half
    to_row = lax.broadcasted_iota(jnp.int32, (size, size), 0)
    from_row = lax.broadcasted_iota(jnp.int32, (size, size), 1)
    wanted = ((to_row >> 1) & 7) * 16 + (to_row >> 4) * 2 + (to_row & 1)
    shuffle = (from_row == wanted).astype(F32).astype(BF16)
    for n in range(nc):
        base_copy(n).wait_recv()
        own_acc[n] = own_acc[n] + base_recv[n]
    expand_local.wait()
    expand_remote.wait_recv()
    s_copy.wait_recv()
    own_sum = s_acc[:lanes] + s_recv[lanes:, :rows]
    sib_sum = s_acc[lanes:] + s_recv[:lanes, :rows]
    shrunk = jnp.concatenate([own_sum, sib_sum], axis=0)
    spread = jnp.where(slot == row_ref[...], shrunk, 0.0).astype(BF16)
    own_spread = lax.dot_general(
        order[:half], spread, NT, preferred_element_type=F32
    ).astype(BF16)

    def finish(n, c):
        columns = pl.ds(pl.multiple_of(n * cw, cw), cw)
        delta = jnp.dot(own_spread, exp[:, columns], preferred_element_type=F32)
        vbuf[n] = (own_acc[n] + delta).astype(BF16)
        return c

    lax.fori_loop(0, nc, finish, 0)

    moved = jnp.dot(shuffle, vbuf[...].reshape(size, cw), preferred_element_type=F32)
    rs_send[...] = moved.astype(BF16).reshape(chips, half, cw)

    def rs_copy(k):
        other = lax.rem(chip + k, chips)
        return to(
            other * 2 + core, rs_send.at[other], rs_recv.at[chip], r_send.at[k], r_recv.at[chip]
        )

    for k in range(1, chips):
        rs_copy(k).start()
    total = rs_send[chip].astype(F32)
    for k in range(1, chips):
        source = lax.rem(chip + k, chips)
        to(sibling, rs_send.at[source], rs_recv.at[source], r_send.at[k], r_recv.at[source]).wait_recv()
        total = total + rs_recv[source].astype(F32)
    for q in range(nc):
        out_ref[:, q * cw:(q + 1) * cw] = total[2 * q:2 * q + 2].astype(BF16)

    for k in range(1, chips):
        rs_copy(k).wait_send()
    s_copy.wait_send()
    expand_remote.wait_send()
    for m in range(chips):
        shrink_remote(m).wait_send()
    for n in range(nc):
        base_copy(n).wait_send()
    for z0 in range(nz):
        when((z0 <= z) & (z < nz - 1), lambda: g_copy(0, z0, y).wait_send())
        when((z0 >= z) & (z > 0), lambda: g_copy(1, z0, y).wait_send())
        g_copy(2, z0, y).wait_send()


def fused_on_device(
    nz, hidden, down_matrix, adapter_shrink, adapter_expand, row_adapter_index, slot_adapter_index
):
    slots, rank, units = adapter_shrink.shape
    rows, width = hidden.shape
    model = down_matrix.shape[1]
    chips = 2 * nz
    lanes = slots * rank
    nc = chips
    cw = model // nc
    half = rows // 2
    vmem = pl.BlockSpec(memory_space=pltpu.VMEM)
    anywhere = pl.BlockSpec(memory_space=pl.ANY)
    dma = pltpu.SemaphoreType.DMA
    return pl.pallas_call(
        functools.partial(kernel, nz, rank, slots),
        out_shape=jax.ShapeDtypeStruct((rows // (2 * chips), model), BF16),
        in_specs=[
            vmem, pl.BlockSpec(memory_space=pltpu.SMEM), anywhere, anywhere, anywhere, anywhere,
        ],
        out_specs=vmem,
        scratch_shapes=[
            pltpu.VMEM((nc, width, cw), BF16),
            pltpu.VMEM((chips, rows, width), BF16),
            pltpu.VMEM((chips, 2 * lanes, width), BF16),
            pltpu.VMEM((2 * lanes, model), BF16),
            pltpu.VMEM((nc, half, cw), F32),
            pltpu.VMEM((nc, half, cw), F32),
            pltpu.VMEM((nc, half, cw), F32),
            pltpu.VMEM((2 * lanes, rows), F32),
            pltpu.VMEM((2 * lanes, 128), F32),
            pltpu.VMEM((2 * lanes, 128), F32),
            pltpu.VMEM((nc, half, cw), BF16),
            pltpu.VMEM((chips, half, cw), BF16),
            pltpu.VMEM((chips, half, cw), BF16),
            dma((1,)),
            dma((nc,)), dma((chips,)), dma((chips,)), dma((chips,)), dma((3,)),
            dma((3, nz)), dma((chips,)), dma((nc,)), dma((nc,)), dma((2,)),
            dma((chips,)), dma((chips,)),
        ],
        compiler_params=pltpu.CompilerParams(
            collective_id=0, has_side_effects=True, vmem_limit_bytes=56 * 1024 * 1024
        ),
    )(
        row_adapter_index.reshape(1, rows),
        slot_adapter_index,
        hidden,
        down_matrix,
        adapter_shrink.reshape(lanes, units),
        adapter_expand.reshape(lanes, model),
    )


def solution(mesh):
    replicas = mesh.shape["replica"]
    in_specs = (
        P("groups", "replica"),
        P("replica", None),
        P("replica", None, None),
        P("replica", None, None),
        P("groups"),
        P(),
    )
    out_specs = P(("groups", "replica"), None)
    body = functools.partial(fused_on_device, 4) if replicas == 16 else plain_on_device
    return jax.shard_map(
        body, mesh=mesh, in_specs=in_specs, out_specs=out_specs, check_vma=False
    )
```
